256 devices in a mesh: req: 8 (over z), ctx: 32 (over x, y, core).
Axes of the slice: x: 4, y: 4, z: 8, core: 2. Of those that a mesh axis runs over, the one named last changes fastest.
Arguments:
- prompt_key_value: bfloat16 [32768, 2048], P('ctx'), may hold values from -6 to 6
- suffix_key_value: bfloat16 [128, 1024, 2048], P('req', 'ctx'), may hold values from -8 to 8
- roots: int32 [128], replicated, may hold values from 0 to 127, as said below
- parents: int32 [3, 128], P(None, 'req'), may hold values from 0 to 15
- block_mask: int32 [128, 8], P('req'), may hold values 0 or 1
- queries: bfloat16 [4, 128, 8192], P(None, 'req', 'ctx'), may hold values from -470 to 470
- draft_kv: bfloat16 [4, 128, 2048], P(None, 'req'), may hold values from -6 to 6
Outputs:
- attention: bfloat16 [4, 128, 8192], P(None, 'req', 'ctx')
The draws below stay inside these ranges and needn't reach their ends.
Inputs may be any that keep to these rules, and one draw needn't show every extreme that they name: The 16 step-0 particles of req index d (d * 16 to d * 16 + 15) contain exactly 2 whose roots r lie on each req index r // 16.
All inputs are finite; a program needn't handle non-finite values. No bound on the sum of `block_mask` on one device may be relied on, other than what follows from the above.
Results may differ from the reference program's by a relative error of at most 0.0034.
Values may be sent and summed in bfloat16 or wider, within the bound.
A program may use at most 192 MiB of HBM per device.

```python
import math
import jax
import jax.numpy as jnp
from jax import lax

QUERY_HEAD_COUNT = 64
KEY_VALUE_HEADS = 8
HEAD_SIZE = 128
DRAFT_STEPS = 4
BLK = 128
PR = 16
PROMPT_DEV = 1024
PARTICLE_COUNT = 128
CAP = 2
SUFFIX_LENGTH = 1024
NSB = 8
PROMPT_LENGTH = 32768


def draft_token_entries(key):
    unsorted_entries = jax.random.normal(jax.random.fold_in(key, 11), (DRAFT_STEPS, PARTICLE_COUNT, 2 * KEY_VALUE_HEADS * HEAD_SIZE), jnp.float32)
    return jnp.clip(unsorted_entries, -6.0, 6.0)


def draw_draft_kv(key, part):
    return draft_token_entries(key).astype(jnp.bfloat16)


def draw_queries(key, part):
    particle_keys = draft_token_entries(key)[:, :, :KEY_VALUE_HEADS * HEAD_SIZE].reshape(DRAFT_STEPS, PARTICLE_COUNT, KEY_VALUE_HEADS, 1, HEAD_SIZE)
    aligned_rows = jnp.broadcast_to(particle_keys, (DRAFT_STEPS, PARTICLE_COUNT, KEY_VALUE_HEADS, QUERY_HEAD_COUNT // KEY_VALUE_HEADS, HEAD_SIZE)).reshape(DRAFT_STEPS, PARTICLE_COUNT, QUERY_HEAD_COUNT * HEAD_SIZE)
    noise = 2.5 * jnp.clip(jax.random.normal(jax.random.fold_in(key, 23), (DRAFT_STEPS, PARTICLE_COUNT, QUERY_HEAD_COUNT * HEAD_SIZE), jnp.float32), -6.0, 6.0)
    return (noise + 1.2 * aligned_rows).astype(jnp.bfloat16)


def draw_roots(key, part):
    req_total = PARTICLE_COUNT // PR
    anchor_list = jnp.repeat(jnp.arange(req_total, dtype=jnp.int32), CAP, total_repeat_length=PR)
    draw_keys = jax.random.split(key, req_total)

    def shuffle_one(subkey):
        return jax.random.permutation(subkey, anchor_list)
    shuffled = jax.vmap(shuffle_one)(draw_keys)
    offsets = jax.random.randint(jax.random.fold_in(key, 7), (req_total, PR), 0, PR, dtype=jnp.int32)
    return (shuffled * PR + offsets).reshape(PARTICLE_COUNT).astype(jnp.int32)


def place_ends(values, stream_key, low, top_value):
    index_at = [jax.random.randint(jax.random.fold_in(stream_key, axis), (), 0, length) for axis, length in enumerate(values.shape)]
    longest = values.shape.index(max(values.shape))
    next_to = index_at[:longest] + [(index_at[longest] + 1) % values.shape[longest]] + index_at[longest + 1:]
    return values.at[tuple(index_at)].set(low).at[tuple(next_to)].set(top_value)


def steps_of(own_key, extent, shards, least, largest):
    def one(axis_at, shards_of):
        steps = jax.random.uniform(jax.random.fold_in(jax.random.fold_in(own_key, 6), axis_at), (shards_of,), jnp.float32, least / len(shards), largest / len(shards))
        return jnp.repeat(jnp.exp(steps), extent[axis_at] // shards_of).reshape((-1,) + (1,) * (len(extent) - axis_at - 1))

    gain = one(*shards[0])
    for cut in shards[1:]:
        gain = gain * one(*cut)
    return gain


def normal_values(rng, shape, scale, limit, cuts=(), kind=jnp.bfloat16):
    level = steps_of(rng, shape, cuts, -0.22, 0.18) if cuts else 1.0
    drawn = jax.random.normal(rng, shape, jnp.float32) * scale * level
    return jnp.minimum(jnp.maximum(drawn, -limit), limit).astype(kind)


def setup_inputs(seed: int = 0) -> dict:
    key_of = jax.random.split(jax.random.key(seed), 8)
    prompt_key_value = normal_values(key_of[0], (PROMPT_LENGTH, 2 * KEY_VALUE_HEADS * HEAD_SIZE), 1.0, 6.0, ((0, 32),))
    suffix_key_value = normal_values(key_of[1], (PARTICLE_COUNT, SUFFIX_LENGTH, 2 * KEY_VALUE_HEADS * HEAD_SIZE), 1.3, 8.0, ((0, 8), (1, 32)))
    roots = draw_roots(jax.random.fold_in(key_of[7], 71), 0)
    parents = place_ends(jax.random.randint(key_of[3], (DRAFT_STEPS - 1, PARTICLE_COUNT), 0, PR), jax.random.fold_in(key_of[3], 1), 0, PR - 1).astype(jnp.int32)
    block_mask = place_ends((jax.random.randint(key_of[4], (PARTICLE_COUNT, NSB), 0, 2) < 1).astype(jnp.int32), jax.random.fold_in(key_of[4], 1), 0, 1)
    queries = draw_queries(jax.random.fold_in(key_of[7], 71), 0)
    draft_kv = draw_draft_kv(jax.random.fold_in(key_of[7], 71), 0)
    return dict(prompt_key_value=prompt_key_value, suffix_key_value=suffix_key_value, roots=roots, parents=parents, block_mask=block_mask, queries=queries, draft_kv=draft_kv)


masked_score = -1e+30

def settle(weight):
    return lax.optimization_barrier(weight.astype(jnp.bfloat16)).astype(jnp.float32)

def reference(prompt_key_value, suffix_key_value, roots, parents, block_mask, queries, draft_kv):
    query_group_size = QUERY_HEAD_COUNT // KEY_VALUE_HEADS
    key_value_width = KEY_VALUE_HEADS * HEAD_SIZE
    score_scale = 1.0 / math.sqrt(HEAD_SIZE)
    block_count = PROMPT_LENGTH // PROMPT_DEV
    suffix_span = SUFFIX_LENGTH // block_count
    particles = jnp.arange(PARTICLE_COUNT, dtype=jnp.int32)
    base_index = particles // PR * PR
    layers_all = []
    for target in range(DRAFT_STEPS):
        current = particles
        columns = [particles] * DRAFT_STEPS
        for back in range(target - 1, -1, -1):
            current = base_index + jnp.take(parents[back], current).astype(jnp.int32)
            columns[back] = current
        layers_all.append(jnp.stack(columns))
    lineage = jnp.stack(layers_all)
    first_step = lineage[:, 0, :]
    sources = jnp.take(roots, first_step).astype(jnp.int32)
    block_ids = jnp.arange(SUFFIX_LENGTH, dtype=jnp.int32) // BLK
    live_tokens = jnp.take(jnp.take(block_mask, first_step, axis=0), block_ids, axis=2) > 0
    draft_token_rows = draft_kv[jnp.arange(DRAFT_STEPS, dtype=jnp.int32)[None, :, None], lineage]
    allowed = jnp.arange(DRAFT_STEPS, dtype=jnp.int32)[None, :] <= jnp.arange(DRAFT_STEPS, dtype=jnp.int32)[:, None]
    query_matrix = queries.reshape(DRAFT_STEPS, PARTICLE_COUNT, KEY_VALUE_HEADS, query_group_size, HEAD_SIZE)

    def head_outputs(current_head_index):
        key_start = current_head_index * HEAD_SIZE
        key_prompt = lax.dynamic_slice_in_dim(prompt_key_value, key_start, HEAD_SIZE, 1).astype(jnp.float32).reshape(block_count, PROMPT_DEV, HEAD_SIZE)
        value_prompt = lax.dynamic_slice_in_dim(prompt_key_value, key_value_width + key_start, HEAD_SIZE, 1).astype(jnp.float32).reshape(block_count, PROMPT_DEV, HEAD_SIZE)
        key_suffix = lax.dynamic_slice_in_dim(suffix_key_value, key_start, HEAD_SIZE, 2)
        value_suffix = lax.dynamic_slice_in_dim(suffix_key_value, key_value_width + key_start, HEAD_SIZE, 2)
        key_draft = lax.dynamic_slice_in_dim(draft_token_rows, key_start, HEAD_SIZE, 3)
        value_draft = lax.dynamic_slice_in_dim(draft_token_rows, key_value_width + key_start, HEAD_SIZE, 3)
        query_head = lax.dynamic_index_in_dim(query_matrix, current_head_index, 2, keepdims=False)

        def per_step(target):
            query_rows = lax.dynamic_index_in_dim(query_head, target, 0, keepdims=False).astype(jnp.float32)
            source_rows = lax.dynamic_index_in_dim(sources, target, 0, keepdims=False)
            live_rows = lax.dynamic_index_in_dim(live_tokens, target, 0, keepdims=False).reshape(PARTICLE_COUNT, block_count, suffix_span)
            keys_here = jnp.take(key_suffix, source_rows, axis=0).astype(jnp.float32).reshape(PARTICLE_COUNT, block_count, suffix_span, HEAD_SIZE)
            values_here = jnp.take(value_suffix, source_rows, axis=0).astype(jnp.float32).reshape(PARTICLE_COUNT, block_count, suffix_span, HEAD_SIZE)
            draft_keys = lax.dynamic_index_in_dim(key_draft, target, 0, keepdims=False).astype(jnp.float32)
            draft_value_rows = lax.dynamic_index_in_dim(value_draft, target, 0, keepdims=False).astype(jnp.float32)
            allowed_row = lax.dynamic_index_in_dim(allowed, target, 0, keepdims=False)
            score_prompt = jnp.einsum('qgd,cnd->qgcn', query_rows, key_prompt) * score_scale
            score_suffix = jnp.einsum('qgd,qcnd->qgcn', query_rows, keys_here) * score_scale
            score_suffix = jnp.where(live_rows[:, None, :, :], score_suffix, masked_score)
            score_draft = jnp.einsum('qgd,sqd->qgs', query_rows, draft_keys) * score_scale
            score_draft = jnp.where(allowed_row[None, None, :], score_draft, masked_score)
            block_peak = jnp.maximum(lax.optimization_barrier(jnp.max(score_prompt, axis=3)), lax.optimization_barrier(jnp.max(score_suffix, axis=3)))
            weight_prompt = jnp.exp(score_prompt - block_peak[..., None])
            weight_suffix = jnp.exp(score_suffix - block_peak[..., None])
            block_total = lax.optimization_barrier(jnp.sum(weight_prompt, axis=3)) + lax.optimization_barrier(jnp.sum(weight_suffix, axis=3))
            block_sum = jnp.einsum('qgcn,cnd->qgcd', settle(weight_prompt), value_prompt)
            block_sum = block_sum + jnp.einsum('qgcn,qcnd->qgcd', settle(weight_suffix), values_here)
            highest = jnp.maximum(lax.optimization_barrier(jnp.max(block_peak, axis=2)), lax.optimization_barrier(jnp.max(score_draft, axis=2)))
            factor = jnp.exp(block_peak - highest[..., None])
            weight_draft = jnp.exp(score_draft - highest[..., None])
            total = lax.optimization_barrier(jnp.sum(block_total * factor, axis=2)) + lax.optimization_barrier(jnp.sum(weight_draft, axis=2))
            accum = lax.optimization_barrier(jnp.sum(block_sum * factor[..., None], axis=2))
            accum = accum + jnp.einsum('qgs,sqd->qgd', settle(weight_draft), draft_value_rows)
            return (accum / total[..., None]).astype(jnp.bfloat16)
        return lax.map(per_step, jnp.arange(DRAFT_STEPS, dtype=jnp.int32))
    output_heads = lax.map(head_outputs, jnp.arange(KEY_VALUE_HEADS, dtype=jnp.int32))
    return jnp.transpose(output_heads, (1, 2, 0, 3, 4)).reshape(DRAFT_STEPS, PARTICLE_COUNT, QUERY_HEAD_COUNT * HEAD_SIZE)
```

```python
import functools
import math

import jax
import jax.numpy as jnp
from jax import lax
from jax.experimental import pallas as pl
from jax.experimental.pallas import tpu as pltpu
from jax.sharding import PartitionSpec as P

MESH = pl.DeviceIdType.MESH

QUERY_HEAD_COUNT = 64
KEY_VALUE_HEADS = 8
HEAD_SIZE = 128
DRAFT_STEPS = 4
WIDTH = KEY_VALUE_HEADS * HEAD_SIZE
REQ = 8
CTX = 32
PER_REQ = 16
CAP = 2
SPAN = 32
PROMPT = 1024
TOKENS = DRAFT_STEPS * PER_REQ
ROWS = 2 * TOKENS
OWNERS = CTX // KEY_VALUE_HEADS
STAT = 8
MASKED = -1e30
EXP_SCALE = math.log2(math.e) / math.sqrt(HEAD_SIZE)


def nt_dot(a, b):
    return lax.dot_general(a, b, (((1,), (1,)), ((), ())), preferred_element_type=jnp.float32)


def kernel(
    roots, parents, block_mask, queries_hbm, draft_hbm, prompt_hbm, suffix_hbm, out_ref,
    prompt, suffix, draft, query_in, zsend, zrecv, query_all, rsend, rrecv, mask, pick, slot,
    load_sem, zs_sem, zr_sem, qs_sem, qr_sem, rs_sem, rr_sem,
):
    z = lax.axis_index("req")
    c = lax.axis_index("ctx")
    group = c // OWNERS

    barrier = pltpu.get_barrier_semaphore()

    def greet_z(i, _):
        pl.semaphore_signal(barrier, inc=1, device_id=(lax.rem(z + i, REQ), c), device_id_type=MESH)
        return 0

    def greet_ctx(i, _):
        pl.semaphore_signal(barrier, inc=1, device_id=(z, lax.rem(c + i, CTX)), device_id_type=MESH)
        return 0

    lax.fori_loop(1, REQ, greet_z, 0)
    lax.fori_loop(1, CTX, greet_ctx, 0)

    load_suffix = pltpu.make_async_copy(suffix_hbm, suffix, load_sem.at[0])
    load_query = pltpu.make_async_copy(queries_hbm, query_in, load_sem.at[1])
    load_prompt = pltpu.make_async_copy(prompt_hbm, prompt, load_sem.at[2])
    load_draft = pltpu.make_async_copy(draft_hbm, draft, load_sem.at[3])
    load_suffix.start()
    load_query.start()
    load_prompt.start()
    load_draft.start()

    def choose(d, _):
        count, first, second = jnp.int32(0), jnp.int32(0), jnp.int32(0)
        for j in range(PER_REQ):
            root = roots[d * PER_REQ + j]
            mine = (root >> 4) == z
            local = root & 15
            first = jnp.where(mine & (count == 0), local, first)
            second = jnp.where(mine & (count == 1), local, second)
            count = count + mine.astype(jnp.int32)
        pick[2 * d] = first
        pick[2 * d + 1] = second
        return 0

    lax.fori_loop(0, REQ, choose, 0)

    load_query.wait()
    query_all[c, 0:TOKENS, :] = query_in[:, 0:HEAD_SIZE]
    query_all[c, TOKENS:ROWS, :] = query_in[:, HEAD_SIZE : 2 * HEAD_SIZE]
    load_suffix.wait()

    def head_of(k):
        return lax.rem(group + 1 + k, KEY_VALUE_HEADS)

    def pack(k):
        key_at = pl.ds(pl.multiple_of(head_of(k) * HEAD_SIZE, HEAD_SIZE), HEAD_SIZE)
        value_at = pl.ds(pl.multiple_of(WIDTH + head_of(k) * HEAD_SIZE, HEAD_SIZE), HEAD_SIZE)

        def one(d, _):
            for s in range(CAP):
                index = pick[2 * d + s]
                zsend[k, d, 0, s * SPAN : (s + 1) * SPAN, :] = suffix[index, :, key_at]
                zsend[k, d, 1, s * SPAN : (s + 1) * SPAN, :] = suffix[index, :, value_at]
            return 0

        lax.fori_loop(0, REQ, one, 0)
        zrecv[k, z] = zsend[k, z]

    def z_copy(k, i):
        d = lax.rem(z + i, REQ)
        return pltpu.make_async_remote_copy(
            src_ref=zsend.at[k, d],
            dst_ref=zrecv.at[k, z],
            send_sem=zs_sem.at[k, d],
            recv_sem=zr_sem.at[k, z],
            device_id=(d, c),
            device_id_type=MESH,
        )

    def z_arrival(k, i):
        s = lax.rem(z + i, REQ)
        return pltpu.make_async_remote_copy(
            src_ref=zsend.at[k, s],
            dst_ref=zrecv.at[k, s],
            send_sem=zs_sem.at[k, s],
            recv_sem=zr_sem.at[k, s],
            device_id=(s, c),
            device_id_type=MESH,
        )

    def q_copy(to):
        return pltpu.make_async_remote_copy(
            src_ref=query_all.at[c],
            dst_ref=query_all.at[c],
            send_sem=qs_sem.at[to],
            recv_sem=qr_sem.at[c],
            device_id=(z, to),
            device_id_type=MESH,
        )

    def q_arrival(s):
        return pltpu.make_async_remote_copy(
            src_ref=query_all.at[s],
            dst_ref=query_all.at[s],
            send_sem=qs_sem.at[s],
            recv_sem=qr_sem.at[s],
            device_id=(z, s),
            device_id_type=MESH,
        )

    def r_copy(to):
        return pltpu.make_async_remote_copy(
            src_ref=rsend.at[to],
            dst_ref=rrecv.at[c],
            send_sem=rs_sem.at[to],
            recv_sem=rr_sem.at[c],
            device_id=(z, to),
            device_id_type=MESH,
        )

    def r_arrival(s):
        return pltpu.make_async_remote_copy(
            src_ref=rsend.at[s],
            dst_ref=rrecv.at[s],
            send_sem=rs_sem.at[s],
            recv_sem=rr_sem.at[s],
            device_id=(z, s),
            device_id_type=MESH,
        )

    def send_stage(k):
        for i in (4, 3, 5, 2, 6, 1, 7):
            z_copy(k, i).start()

    pack(0)
    pl.semaphore_wait(barrier, REQ - 1 + CTX - 1)
    send_stage(0)

    def send_query(i, _):
        to = lax.rem(group + 2 * KEY_VALUE_HEADS - 1 - i // OWNERS, KEY_VALUE_HEADS) * OWNERS + lax.rem(c + i, OWNERS)

        @pl.when(to != c)
        def _():
            q_copy(to).start()

        return 0

    lax.fori_loop(0, CTX, send_query, 0)

    def pack_and_send(k, _):
        pack(k)
        send_stage(k)
        return 0

    lax.fori_loop(1, KEY_VALUE_HEADS, pack_and_send, 0)

    own = [roots[z * PER_REQ + j] >> 4 for j in range(PER_REQ)]
    for j in range(PER_REQ):
        rank = jnp.int32(0)
        for i in range(j):
            rank = rank + (own[i] == own[j]).astype(jnp.int32)
        slot[j] = own[j] * CAP + rank

    lane_slot = lax.broadcasted_iota(jnp.int32, (1, REQ * CAP * SPAN), 1) // SPAN
    lane_token = lax.rem(lax.broadcasted_iota(jnp.int32, (1, ROWS), 1), TOKENS)

    def trace(j, carry):
        lines = list(carry)
        for t in range(DRAFT_STEPS):
            at = j
            path = {t: at}
            for back in range(t - 1, -1, -1):
                at = parents[back, at]
                path[back] = at
            here = jnp.where(block_mask[at, group] > 0, slot[at], -1)
            mask[pl.ds(t * PER_REQ + j, 1), :] = jnp.where(lane_slot == here, 0.0, MASKED)
            for s in range(t + 1):
                lines[s] = jnp.where(lane_token == t * PER_REQ + j, path[s], lines[s])
        return tuple(lines)

    lines = lax.fori_loop(
        0, PER_REQ, trace, tuple(jnp.full((1, ROWS), -1, jnp.int32) for _ in range(DRAFT_STEPS))
    )

    load_prompt.wait()
    load_draft.wait()
    lane = lax.broadcasted_iota(jnp.int32, (ROWS, HEAD_SIZE), 1)

    def stage(k, _):
        h = head_of(k)
        key_at = pl.ds(pl.multiple_of(h * HEAD_SIZE, HEAD_SIZE), HEAD_SIZE)
        value_at = pl.ds(pl.multiple_of(WIDTH + h * HEAD_SIZE, HEAD_SIZE), HEAD_SIZE)

        def wait_z(i, _):
            z_arrival(k, i).wait_recv()
            return 0

        lax.fori_loop(1, REQ, wait_z, 0)

        def chunk(part, _):
            owner = h * OWNERS + part

            @pl.when(owner != c)
            def _():
                q_arrival(owner).wait_recv()

            rows = query_all[owner]
            score_prompt = nt_dot(rows, prompt[:, key_at])
            keys = zrecv[k, :, 0].reshape(REQ * CAP * SPAN, HEAD_SIZE)
            values = zrecv[k, :, 1].reshape(REQ * CAP * SPAN, HEAD_SIZE)
            bias = mask[...]
            score_suffix = nt_dot(rows, keys) + jnp.concatenate([bias, bias], axis=0)
            peak = jnp.maximum(
                jnp.max(score_prompt, axis=1, keepdims=True), jnp.max(score_suffix, axis=1, keepdims=True)
            )
            weight_prompt = jnp.exp2((score_prompt - peak) * EXP_SCALE)
            weight_suffix = jnp.exp2((score_suffix - peak) * EXP_SCALE)
            total = jnp.sum(weight_prompt, axis=1, keepdims=True) + jnp.sum(weight_suffix, axis=1, keepdims=True)
            accum = jnp.dot(
                weight_prompt.astype(jnp.bfloat16), prompt[:, value_at], preferred_element_type=jnp.float32
            )
            accum = accum + jnp.dot(weight_suffix.astype(jnp.bfloat16), values, preferred_element_type=jnp.float32)
            rsend[owner, 0:ROWS, :] = accum
            stats = jnp.transpose(jnp.where(lane == 0, peak, total))
            rsend[owner, ROWS : ROWS + STAT, :] = stats[0:STAT]

            @pl.when(owner != c)
            def _():
                r_copy(owner).start()

            return 0

        lax.fori_loop(0, OWNERS, chunk, 0)
        return 0

    lax.fori_loop(0, KEY_VALUE_HEADS, stage, 0)

    rrecv[c] = rsend[c]

    key_at = pl.ds(pl.multiple_of(group * HEAD_SIZE, HEAD_SIZE), HEAD_SIZE)
    value_at = pl.ds(pl.multiple_of(WIDTH + group * HEAD_SIZE, HEAD_SIZE), HEAD_SIZE)
    score_draft = nt_dot(draft[:, key_at], query_all[c])
    particle = lax.broadcasted_iota(jnp.int32, (PER_REQ, ROWS), 0)
    allowed = jnp.concatenate([jnp.where(particle == line, 1, 0) for line in lines], axis=0)
    score_draft = jnp.where(allowed > 0, score_draft, MASKED)

    def wait_r(i, _):
        r_arrival(lax.rem(c + i, CTX)).wait_recv()
        return 0

    lax.fori_loop(1, CTX, wait_r, 0)

    peaks = rrecv[:, ROWS, :]
    totals = rrecv[:, ROWS + 1, :]
    highest = jnp.maximum(jnp.max(peaks, axis=0, keepdims=True), jnp.max(score_draft, axis=0, keepdims=True))
    factor = jnp.exp2((peaks - highest) * EXP_SCALE)
    weight_draft = jnp.exp2((score_draft - highest) * EXP_SCALE)
    total = jnp.sum(totals * factor, axis=0, keepdims=True) + jnp.sum(weight_draft, axis=0, keepdims=True)
    turned = jnp.transpose(
        jnp.concatenate([factor, jnp.broadcast_to(total, (CTX, ROWS)), weight_draft], axis=0)
    )
    numerator = jnp.dot(
        turned[:, 2 * CTX :].astype(jnp.bfloat16), draft[:, value_at], preferred_element_type=jnp.float32
    )
    for s in range(CTX):
        numerator = numerator + rrecv[s, 0:ROWS, :] * turned[:, s : s + 1]
    result = (numerator / turned[:, CTX : CTX + 1]).astype(jnp.bfloat16)
    out_ref[:, 0:HEAD_SIZE] = result[0:TOKENS]
    out_ref[:, HEAD_SIZE : 2 * HEAD_SIZE] = result[TOKENS:ROWS]

    def drain_z(k, _):
        def one(i, _):
            z_copy(k, i).wait_send()
            return 0

        return lax.fori_loop(1, REQ, one, 0)

    lax.fori_loop(0, KEY_VALUE_HEADS, drain_z, 0)

    def drain_ctx(i, _):
        to = lax.rem(c + i, CTX)
        q_copy(to).wait_send()
        r_copy(to).wait_send()
        return 0

    lax.fori_loop(1, CTX, drain_ctx, 0)


def body(prompt_key_value, suffix_key_value, roots, parents, block_mask, queries, draft_kv):
    smem = pl.BlockSpec(memory_space=pltpu.SMEM)
    anywhere = pl.BlockSpec(memory_space=pl.ANY)
    bf16, f32 = jnp.bfloat16, jnp.float32
    result = pl.pallas_call(
        kernel,
        out_shape=jax.ShapeDtypeStruct((TOKENS, 2 * HEAD_SIZE), bf16),
        in_specs=[smem, smem, smem, anywhere, anywhere, anywhere, anywhere],
        out_specs=pl.BlockSpec(memory_space=pltpu.VMEM),
        scratch_shapes=[
            pltpu.VMEM((PROMPT, 2 * WIDTH), bf16),
            pltpu.VMEM((PER_REQ, SPAN, 2 * WIDTH), bf16),
            pltpu.VMEM((TOKENS, 2 * WIDTH), bf16),
            pltpu.VMEM((TOKENS, 2 * HEAD_SIZE), bf16),
            pltpu.VMEM((KEY_VALUE_HEADS, REQ, 2, CAP * SPAN, HEAD_SIZE), bf16),
            pltpu.VMEM((KEY_VALUE_HEADS, REQ, 2, CAP * SPAN, HEAD_SIZE), bf16),
            pltpu.VMEM((CTX, ROWS, HEAD_SIZE), bf16),
            pltpu.VMEM((CTX, ROWS + STAT, HEAD_SIZE), f32),
            pltpu.VMEM((CTX, ROWS + STAT, HEAD_SIZE), f32),
            pltpu.VMEM((TOKENS, REQ * CAP * SPAN), f32),
            pltpu.SMEM((REQ * CAP,), jnp.int32),
            pltpu.SMEM((PER_REQ,), jnp.int32),
            pltpu.SemaphoreType.DMA((4,)),
            pltpu.SemaphoreType.DMA((KEY_VALUE_HEADS, REQ)),
            pltpu.SemaphoreType.DMA((KEY_VALUE_HEADS, REQ)),
            pltpu.SemaphoreType.DMA((CTX,)),
            pltpu.SemaphoreType.DMA((CTX,)),
            pltpu.SemaphoreType.DMA((CTX,)),
            pltpu.SemaphoreType.DMA((CTX,)),
        ],
        compiler_params=pltpu.CompilerParams(
            collective_id=0, has_side_effects=True, vmem_limit_bytes=48 * 1024 * 1024
        ),
        cost_estimate=pl.CostEstimate(flops=3_300_000_000, bytes_accessed=7_000_000, transcendentals=6_300_000),
    )(
        roots,
        parents,
        block_mask,
        queries.reshape(TOKENS, 2 * HEAD_SIZE),
        draft_kv.reshape(TOKENS, 2 * WIDTH),
        prompt_key_value,
        suffix_key_value,
    )
    return result.reshape(DRAFT_STEPS, PER_REQ, 2 * HEAD_SIZE)


def solution(mesh):
    return jax.shard_map(
        body,
        mesh=mesh,
        in_specs=(
            P("ctx", None),
            P("req", "ctx", None),
            P(),
            P(None, "req"),
            P("req", None),
            P(None, "req", "ctx"),
            P(None, "req", None),
        ),
        out_specs=P(None, "req", "ctx"),
        check_vma=False,
    )
```

```python
import functools
import math

import jax
import jax.numpy as jnp
from jax import lax
from jax.experimental import pallas as pl
from jax.experimental.pallas import tpu as pltpu
from jax.sharding import PartitionSpec as P

MESH = pl.DeviceIdType.MESH

QUERY_HEAD_COUNT = 64
KEY_VALUE_HEADS = 8
HEAD_SIZE = 128
DRAFT_STEPS = 4
WIDTH = KEY_VALUE_HEADS * HEAD_SIZE
REQ = 8
CTX = 32
CHIPS = CTX // 2
PER_REQ = 16
CAP = 2
SPAN = 32
PROMPT = 1024
TOKENS = DRAFT_STEPS * PER_REQ
ROWS = 2 * TOKENS
OWNERS = CTX // KEY_VALUE_HEADS
STAT = 8
MASKED = -1e30
EXP_SCALE = math.log2(math.e) / math.sqrt(HEAD_SIZE)


def nt_dot(a, b):
    return lax.dot_general(a, b, (((1,), (1,)), ((), ())), preferred_element_type=jnp.float32)


def kernel(
    roots_hbm, parents_hbm, mask_hbm, queries_hbm, draft_hbm, prompt_hbm, suffix_hbm, out_ref,
    prompt, suffix, draft, query_in, zsend, zrecv, query_all, xsend, xrecv, keep, rsend, rrecv, mask,
    roots, parents, block_mask, pick, slot,
    load_sem, zs_sem, zr_sem, qs_sem, qf_sem, qr_sem, xs_sem, xr_sem, rs_sem, rr_sem,
):
    z = lax.axis_index("req")
    c = lax.axis_index("ctx")
    group = c // OWNERS
    chip = c // 2
    core = lax.rem(c, 2)
    sibling = chip * 2 + 1 - core

    barrier = pltpu.get_barrier_semaphore()

    def greet_z(i, _):
        pl.semaphore_signal(barrier, inc=1, device_id=(lax.rem(z + i, REQ), c), device_id_type=MESH)
        return 0

    def greet_chip(i, _):
        to = lax.rem(chip + i, CHIPS) * 2 + core
        pl.semaphore_signal(barrier, inc=1, device_id=(z, to), device_id_type=MESH)
        return 0

    lax.fori_loop(1, REQ, greet_z, 0)
    lax.fori_loop(1, CHIPS, greet_chip, 0)
    pl.semaphore_signal(barrier, inc=1, device_id=(z, sibling), device_id_type=MESH)

    load_suffix = pltpu.make_async_copy(suffix_hbm, suffix, load_sem.at[0])
    load_query = pltpu.make_async_copy(queries_hbm, query_in, load_sem.at[1])
    load_prompt = pltpu.make_async_copy(prompt_hbm, prompt, load_sem.at[2])
    load_draft = pltpu.make_async_copy(draft_hbm, draft, load_sem.at[3])
    load_roots = pltpu.make_async_copy(roots_hbm, roots, load_sem.at[4])
    load_parents = pltpu.make_async_copy(parents_hbm, parents, load_sem.at[5])
    load_mask = pltpu.make_async_copy(mask_hbm, block_mask, load_sem.at[6])
    load_roots.start()
    load_suffix.start()
    load_query.start()
    load_parents.start()
    load_mask.start()
    load_prompt.start()
    load_draft.start()

    def choose(d, _):
        count, first, second = jnp.int32(0), jnp.int32(0), jnp.int32(0)
        for j in range(PER_REQ):
            root = roots[d * PER_REQ + j]
            mine = (root >> 4) == z
            local = root & 15
            first = jnp.where(mine & (count == 0), local, first)
            second = jnp.where(mine & (count == 1), local, second)
            count = count + mine.astype(jnp.int32)
        pick[2 * d] = first
        pick[2 * d + 1] = second
        return 0

    load_roots.wait()
    lax.fori_loop(0, REQ, choose, 0)

    load_query.wait()
    query_all[c, 0:TOKENS, :] = query_in[:, 0:HEAD_SIZE]
    query_all[c, TOKENS:ROWS, :] = query_in[:, HEAD_SIZE : 2 * HEAD_SIZE]
    load_suffix.wait()

    def head_of(k):
        return lax.rem(group + 1 + k, KEY_VALUE_HEADS)

    def pack(k):
        key_at = pl.ds(pl.multiple_of(head_of(k) * HEAD_SIZE, HEAD_SIZE), HEAD_SIZE)
        value_at = pl.ds(pl.multiple_of(WIDTH + head_of(k) * HEAD_SIZE, HEAD_SIZE), HEAD_SIZE)

        def one(d, _):
            for s in range(CAP):
                index = pick[2 * d + s]
                zsend[k, d, 0, s * SPAN : (s + 1) * SPAN, :] = suffix[index, :, key_at]
                zsend[k, d, 1, s * SPAN : (s + 1) * SPAN, :] = suffix[index, :, value_at]
            return 0

        lax.fori_loop(0, REQ, one, 0)
        zrecv[k, z] = zsend[k, z]

    def z_copy(k, i):
        d = lax.rem(z + i, REQ)
        return pltpu.make_async_remote_copy(
            src_ref=zsend.at[k, d],
            dst_ref=zrecv.at[k, z],
            send_sem=zs_sem.at[k, d],
            recv_sem=zr_sem.at[k, z],
            device_id=(d, c),
            device_id_type=MESH,
        )

    def z_arrival(k, i):
        s = lax.rem(z + i, REQ)
        return pltpu.make_async_remote_copy(
            src_ref=zsend.at[k, s],
            dst_ref=zrecv.at[k, s],
            send_sem=zs_sem.at[k, s],
            recv_sem=zr_sem.at[k, s],
            device_id=(s, c),
            device_id_type=MESH,
        )

    def q_send(source, to, sem):
        return pltpu.make_async_remote_copy(
            src_ref=query_all.at[source],
            dst_ref=query_all.at[source],
            send_sem=sem,
            recv_sem=qr_sem.at[source],
            device_id=(z, to),
            device_id_type=MESH,
        )

    def q_copy(to):
        return q_send(c, to, qs_sem.at[to])

    def q_forward(source):
        return q_send(source, sibling, qf_sem.at[source])

    def x_copy(k, half):
        return pltpu.make_async_remote_copy(
            src_ref=xsend.at[k, half],
            dst_ref=xrecv.at[k, half],
            send_sem=xs_sem.at[k, half],
            recv_sem=xr_sem.at[k, half],
            device_id=(z, sibling),
            device_id_type=MESH,
        )

    def r_copy(to_chip):
        return pltpu.make_async_remote_copy(
            src_ref=rsend.at[to_chip],
            dst_ref=rrecv.at[chip],
            send_sem=rs_sem.at[to_chip],
            recv_sem=rr_sem.at[chip],
            device_id=(z, to_chip * 2 + core),
            device_id_type=MESH,
        )

    def r_arrival(from_chip):
        return pltpu.make_async_remote_copy(
            src_ref=rsend.at[from_chip],
            dst_ref=rrecv.at[from_chip],
            send_sem=rs_sem.at[from_chip],
            recv_sem=rr_sem.at[from_chip],
            device_id=(z, from_chip * 2 + core),
            device_id_type=MESH,
        )

    def send_stage(k):
        for i in (4, 3, 5, 2, 6, 1, 7):
            z_copy(k, i).start()

    pack(0)
    pl.semaphore_wait(barrier, REQ - 1 + CHIPS)
    send_stage(0)

    q_copy(sibling).start()

    def send_query(i, _):
        to = lax.rem(group + 2 * KEY_VALUE_HEADS - 1 - i // 2, KEY_VALUE_HEADS) * 2 + lax.rem(chip + i, 2)

        @pl.when(to != chip)
        def _():
            q_copy(to * 2 + core).start()

        return 0

    lax.fori_loop(0, CHIPS, send_query, 0)

    def pack_and_send(k, _):
        pack(k)
        send_stage(k)
        return 0

    lax.fori_loop(1, KEY_VALUE_HEADS, pack_and_send, 0)

    load_parents.wait()
    load_mask.wait()

    own = [roots[z * PER_REQ + j] >> 4 for j in range(PER_REQ)]
    for j in range(PER_REQ):
        rank = jnp.int32(0)
        for i in range(j):
            rank = rank + (own[i] == own[j]).astype(jnp.int32)
        slot[j] = own[j] * CAP + rank

    lane_slot = lax.broadcasted_iota(jnp.int32, (1, REQ * CAP * SPAN), 1) // SPAN
    lane_token = lax.rem(lax.broadcasted_iota(jnp.int32, (1, ROWS), 1), TOKENS)

    def trace(j, carry):
        lines = list(carry)
        for t in range(DRAFT_STEPS):
            at = j
            path = {t: at}
            for back in range(t - 1, -1, -1):
                at = parents[back, at]
                path[back] = at
            here = jnp.where(block_mask[group, at] > 0, slot[at], -1)
            mask[pl.ds(t * PER_REQ + j, 1), :] = jnp.where(lane_slot == here, 0.0, MASKED)
            for s in range(t + 1):
                lines[s] = jnp.where(lane_token == t * PER_REQ + j, path[s], lines[s])
        return tuple(lines)

    lines = lax.fori_loop(
        0, PER_REQ, trace, tuple(jnp.full((1, ROWS), -1, jnp.int32) for _ in range(DRAFT_STEPS))
    )

    load_prompt.wait()
    load_draft.wait()
    lane = lax.broadcasted_iota(jnp.int32, (ROWS, HEAD_SIZE), 1)

    def hand_on(k):
        for half in range(2):
            owner = head_of(k) * OWNERS + core + 2 * half

            @pl.when(owner != c)
            def _():
                q_send(owner, sibling, qf_sem.at[owner]).wait_recv()
                q_forward(owner).start()

    def partial(k, owner):
        h = head_of(k)
        key_at = pl.ds(pl.multiple_of(h * HEAD_SIZE, HEAD_SIZE), HEAD_SIZE)
        value_at = pl.ds(pl.multiple_of(WIDTH + h * HEAD_SIZE, HEAD_SIZE), HEAD_SIZE)
        rows = query_all[owner]
        score_prompt = nt_dot(rows, prompt[:, key_at])
        keys = zrecv[k, :, 0].reshape(REQ * CAP * SPAN, HEAD_SIZE)
        values = zrecv[k, :, 1].reshape(REQ * CAP * SPAN, HEAD_SIZE)
        bias = mask[...]
        score_suffix = nt_dot(rows, keys) + jnp.concatenate([bias, bias], axis=0)
        peak = jnp.maximum(
            jnp.max(score_prompt, axis=1, keepdims=True), jnp.max(score_suffix, axis=1, keepdims=True)
        )
        weight_prompt = jnp.exp2((score_prompt - peak) * EXP_SCALE)
        weight_suffix = jnp.exp2((score_suffix - peak) * EXP_SCALE)
        total = jnp.sum(weight_prompt, axis=1, keepdims=True) + jnp.sum(weight_suffix, axis=1, keepdims=True)
        accum = jnp.dot(
            weight_prompt.astype(jnp.bfloat16), prompt[:, value_at], preferred_element_type=jnp.float32
        )
        accum = accum + jnp.dot(weight_suffix.astype(jnp.bfloat16), values, preferred_element_type=jnp.float32)
        return accum, jnp.where(lane == 0, peak, total)

    def stage(k, _):
        @pl.when(k < KEY_VALUE_HEADS - 1)
        def _():
            hand_on(k + 1)

        def wait_z(i, _):
            z_arrival(k, i).wait_recv()
            return 0

        lax.fori_loop(1, REQ, wait_z, 0)

        def give(half, _):
            owner = head_of(k) * OWNERS + 1 - core + 2 * half
            q_send(owner, sibling, qf_sem.at[owner]).wait_recv()
            accum, stats = partial(k, owner)
            xsend[k, half, 0:ROWS, :] = accum
            xsend[k, half, ROWS : 2 * ROWS, :] = stats
            x_copy(k, half).start()
            return 0

        lax.fori_loop(0, 2, give, 0)

        def hold(half, _):
            accum, stats = partial(k, head_of(k) * OWNERS + core + 2 * half)
            keep[half, 0:ROWS, :] = accum
            keep[half, ROWS : 2 * ROWS, :] = stats
            return 0

        lax.fori_loop(0, 2, hold, 0)

        def combine(half, _):
            to_chip = head_of(k) * 2 + half
            x_copy(k, half).wait_recv()
            peak_here, peak_there = keep[half, ROWS : 2 * ROWS, 0:1], xrecv[k, half, ROWS : 2 * ROWS, 0:1]
            total_here, total_there = keep[half, ROWS : 2 * ROWS, 1:2], xrecv[k, half, ROWS : 2 * ROWS, 1:2]
            peak = jnp.maximum(peak_here, peak_there)
            here = jnp.exp2((peak_here - peak) * EXP_SCALE)
            there = jnp.exp2((peak_there - peak) * EXP_SCALE)
            rsend[to_chip, 0:ROWS, :] = keep[half, 0:ROWS, :] * here + xrecv[k, half, 0:ROWS, :] * there
            stats = jnp.transpose(jnp.where(lane == 0, peak, total_here * here + total_there * there))
            rsend[to_chip, ROWS : ROWS + STAT, :] = stats[0:STAT]

            @pl.when(to_chip != chip)
            def _():
                r_copy(to_chip).start()

            return 0

        lax.fori_loop(0, 2, combine, 0)
        return 0

    hand_on(0)
    lax.fori_loop(0, KEY_VALUE_HEADS, stage, 0)

    rrecv[chip] = rsend[chip]

    key_at = pl.ds(pl.multiple_of(group * HEAD_SIZE, HEAD_SIZE), HEAD_SIZE)
    value_at = pl.ds(pl.multiple_of(WIDTH + group * HEAD_SIZE, HEAD_SIZE), HEAD_SIZE)
    score_draft = nt_dot(draft[:, key_at], query_all[c])
    particle = lax.broadcasted_iota(jnp.int32, (PER_REQ, ROWS), 0)
    allowed = jnp.concatenate([jnp.where(particle == line, 1, 0) for line in lines], axis=0)
    score_draft = jnp.where(allowed > 0, score_draft, MASKED)

    def wait_r(i, _):
        r_arrival(lax.rem(chip + i, CHIPS)).wait_recv()
        return 0

    lax.fori_loop(1, CHIPS, wait_r, 0)

    peaks = rrecv[:, ROWS, :]
    totals = rrecv[:, ROWS + 1, :]
    highest = jnp.maximum(jnp.max(peaks, axis=0, keepdims=True), jnp.max(score_draft, axis=0, keepdims=True))
    factor = jnp.exp2((peaks - highest) * EXP_SCALE)
    weight_draft = jnp.exp2((score_draft - highest) * EXP_SCALE)
    total = jnp.sum(totals * factor, axis=0, keepdims=True) + jnp.sum(weight_draft, axis=0, keepdims=True)
    turned = jnp.transpose(
        jnp.concatenate([factor, jnp.broadcast_to(total, (TOKENS - CHIPS, ROWS)), weight_draft], axis=0)
    )
    numerator = jnp.dot(
        turned[:, TOKENS:].astype(jnp.bfloat16), draft[:, value_at], preferred_element_type=jnp.float32
    )
    for s in range(CHIPS):
        numerator = numerator + rrecv[s, 0:ROWS, :] * turned[:, s : s + 1]
    result = (numerator / turned[:, CHIPS : CHIPS + 1]).astype(jnp.bfloat16)
    out_ref[:, 0:HEAD_SIZE] = result[0:TOKENS]
    out_ref[:, HEAD_SIZE : 2 * HEAD_SIZE] = result[TOKENS:ROWS]

    def drain_z(k, _):
        def one(i, _):
            z_copy(k, i).wait_send()
            return 0

        return lax.fori_loop(1, REQ, one, 0)

    lax.fori_loop(0, KEY_VALUE_HEADS, drain_z, 0)

    def drain_chip(i, _):
        to = lax.rem(chip + i, CHIPS)
        q_copy(to * 2 + core).wait_send()
        q_forward(to * 2 + core).wait_send()
        r_copy(to).wait_send()
        return 0

    lax.fori_loop(1, CHIPS, drain_chip, 0)
    q_copy(sibling).wait_send()

    def drain_x(k, _):
        for half in range(2):
            x_copy(k, half).wait_send()
        return 0

    lax.fori_loop(0, KEY_VALUE_HEADS, drain_x, 0)


def body(prompt_key_value, suffix_key_value, roots, parents, block_mask, queries, draft_kv):
    hbm = pl.BlockSpec(memory_space=pltpu.HBM)
    bf16, f32 = jnp.bfloat16, jnp.float32
    result = pl.pallas_call(
        kernel,
        out_shape=jax.ShapeDtypeStruct((TOKENS, 2 * HEAD_SIZE), bf16),
        in_specs=[hbm] * 7,
        out_specs=pl.BlockSpec(memory_space=pltpu.VMEM),
        scratch_shapes=[
            pltpu.VMEM((PROMPT, 2 * WIDTH), bf16),
            pltpu.VMEM((PER_REQ, SPAN, 2 * WIDTH), bf16),
            pltpu.VMEM((TOKENS, 2 * WIDTH), bf16),
            pltpu.VMEM((TOKENS, 2 * HEAD_SIZE), bf16),
            pltpu.VMEM((KEY_VALUE_HEADS, REQ, 2, CAP * SPAN, HEAD_SIZE), bf16),
            pltpu.VMEM((KEY_VALUE_HEADS, REQ, 2, CAP * SPAN, HEAD_SIZE), bf16),
            pltpu.VMEM((CTX, ROWS, HEAD_SIZE), bf16),
            pltpu.VMEM((KEY_VALUE_HEADS, 2, 2 * ROWS, HEAD_SIZE), f32),
            pltpu.VMEM((KEY_VALUE_HEADS, 2, 2 * ROWS, HEAD_SIZE), f32),
            pltpu.VMEM((2, 2 * ROWS, HEAD_SIZE), f32),
            pltpu.VMEM((CHIPS, ROWS + STAT, HEAD_SIZE), f32),
            pltpu.VMEM((CHIPS, ROWS + STAT, HEAD_SIZE), f32),
            pltpu.VMEM((TOKENS, REQ * CAP * SPAN), f32),
            pltpu.SMEM((REQ * PER_REQ,), jnp.int32),
            pltpu.SMEM((DRAFT_STEPS - 1, PER_REQ), jnp.int32),
            pltpu.SMEM((KEY_VALUE_HEADS, PER_REQ), jnp.int32),
            pltpu.SMEM((REQ * CAP,), jnp.int32),
            pltpu.SMEM((PER_REQ,), jnp.int32),
            pltpu.SemaphoreType.DMA((7,)),
            pltpu.SemaphoreType.DMA((KEY_VALUE_HEADS, REQ)),
            pltpu.SemaphoreType.DMA((KEY_VALUE_HEADS, REQ)),
            pltpu.SemaphoreType.DMA((CTX,)),
            pltpu.SemaphoreType.DMA((CTX,)),
            pltpu.SemaphoreType.DMA((CTX,)),
            pltpu.SemaphoreType.DMA((KEY_VALUE_HEADS, 2)),
            pltpu.SemaphoreType.DMA((KEY_VALUE_HEADS, 2)),
            pltpu.SemaphoreType.DMA((CHIPS,)),
            pltpu.SemaphoreType.DMA((CHIPS,)),
        ],
        compiler_params=pltpu.CompilerParams(
            collective_id=0, has_side_effects=True, vmem_limit_bytes=48 * 1024 * 1024
        ),
        cost_estimate=pl.CostEstimate(flops=3_300_000_000, bytes_accessed=7_000_000, transcendentals=6_300_000),
    )(*(
        pltpu.with_memory_space_constraint(operand, pltpu.HBM)
        for operand in (
            roots,
            parents,
            block_mask.T,
            queries.reshape(TOKENS, 2 * HEAD_SIZE),
            draft_kv.reshape(TOKENS, 2 * WIDTH),
            prompt_key_value,
            suffix_key_value,
        )
    ))
    return result.reshape(DRAFT_STEPS, PER_REQ, 2 * HEAD_SIZE)


def solution(mesh):
    return jax.shard_map(
        body,
        mesh=mesh,
        in_specs=(
            P("ctx", None),
            P("req", "ctx", None),
            P(),
            P(None, "req"),
            P("req", None),
            P(None, "req", "ctx"),
            P(None, "req", None),
        ),
        out_specs=P(None, "req", "ctx"),
        check_vma=False,
    )
```

```python
import functools
import math

import jax
import jax.numpy as jnp
from jax import lax
from jax.experimental import pallas as pl
from jax.experimental.pallas import tpu as pltpu
from jax.sharding import PartitionSpec as P

MESH = pl.DeviceIdType.MESH

QUERY_HEAD_COUNT = 64
KEY_VALUE_HEADS = 8
HEAD_SIZE = 128
DRAFT_STEPS = 4
WIDTH = KEY_VALUE_HEADS * HEAD_SIZE
REQ = 8
CTX = 32
CHIPS = CTX // 2
LAST = KEY_VALUE_HEADS - 1
EARLY = 4
PER_REQ = 16
CAP = 2
SPAN = 32
PROMPT = 1024
TOKENS = DRAFT_STEPS * PER_REQ
ROWS = 2 * TOKENS
OWNERS = CTX // KEY_VALUE_HEADS
STAT = 8
MASKED = -1e30
EXP_SCALE = math.log2(math.e) / math.sqrt(HEAD_SIZE)


def nt_dot(a, b):
    return lax.dot_general(a, b, (((1,), (1,)), ((), ())), preferred_element_type=jnp.float32)


def kernel(
    roots_hbm, parents_hbm, mask_hbm, queries_hbm, draft_hbm, prompt_hbm, suffix_hbm, out_ref,
    prompt, suffix, first_pieces, draft, query_in, zsend, zrecv, query_all, xsend, xrecv, keep, rsend, rrecv,
    last_part, lsend, lrecv, base, mask,
    roots, parents, block_mask, pick, slot,
    load_sem, zs_sem, zr_sem, qs_sem, qf_sem, qr_sem, xs_sem, xr_sem, rs_sem, rr_sem, ls_sem, lr_sem,
):
    z = lax.axis_index("req")
    c = lax.axis_index("ctx")
    group = c // OWNERS
    chip = c // 2
    core = lax.rem(c, 2)
    sibling = chip * 2 + 1 - core
    place = lax.rem(c, OWNERS)
    across = group * OWNERS + OWNERS - 1 - place

    def head_of(k):
        return lax.rem(group + 1 + k, KEY_VALUE_HEADS)

    def columns(k):
        key_at = pl.ds(pl.multiple_of(head_of(k) * HEAD_SIZE, HEAD_SIZE), HEAD_SIZE)
        value_at = pl.ds(pl.multiple_of(WIDTH + head_of(k) * HEAD_SIZE, HEAD_SIZE), HEAD_SIZE)
        return key_at, value_at

    load_roots = pltpu.make_async_copy(roots_hbm, roots, load_sem.at[0])
    load_roots.start()
    key_at, value_at = columns(0)
    load_keys = pltpu.make_async_copy(suffix_hbm.at[:, :, key_at], first_pieces.at[0], load_sem.at[1])
    load_values = pltpu.make_async_copy(suffix_hbm.at[:, :, value_at], first_pieces.at[1], load_sem.at[2])
    load_keys.start()
    load_values.start()

    barrier = pltpu.get_barrier_semaphore()

    def greet_z(i, _):
        pl.semaphore_signal(barrier, inc=1, device_id=(lax.rem(z + i, REQ), c), device_id_type=MESH)
        return 0

    def greet_chip(i, _):
        to = lax.rem(chip + i, CHIPS) * 2 + core
        pl.semaphore_signal(barrier, inc=1, device_id=(z, to), device_id_type=MESH)
        return 0

    lax.fori_loop(1, REQ, greet_z, 0)
    lax.fori_loop(1, CHIPS, greet_chip, 0)
    pl.semaphore_signal(barrier, inc=1, device_id=(z, sibling), device_id_type=MESH)
    pl.semaphore_signal(barrier, inc=1, device_id=(z, across), device_id_type=MESH)

    load_query = pltpu.make_async_copy(queries_hbm, query_in, load_sem.at[3])
    load_suffix = pltpu.make_async_copy(suffix_hbm, suffix, load_sem.at[4])
    load_parents = pltpu.make_async_copy(parents_hbm, parents, load_sem.at[5])
    load_mask = pltpu.make_async_copy(mask_hbm, block_mask, load_sem.at[6])
    load_prompt = pltpu.make_async_copy(prompt_hbm, prompt, load_sem.at[7])
    load_draft = pltpu.make_async_copy(draft_hbm, draft, load_sem.at[8])
    load_query.start()
    load_suffix.start()
    load_parents.start()
    load_mask.start()
    load_prompt.start()
    load_draft.start()

    def choose(d, _):
        count, first, second = jnp.int32(0), jnp.int32(0), jnp.int32(0)
        for j in range(PER_REQ):
            root = roots[d * PER_REQ + j]
            mine = (root >> 4) == z
            local = root & 15
            first = jnp.where(mine & (count == 0), local, first)
            second = jnp.where(mine & (count == 1), local, second)
            count = count + mine.astype(jnp.int32)
        pick[2 * d] = first
        pick[2 * d + 1] = second
        return 0

    load_roots.wait()
    lax.fori_loop(0, REQ, choose, 0)

    def pack(k, keys_of, values_of):
        def one(d, _):
            for s in range(CAP):
                index = pick[2 * d + s]
                zsend[k, d, 0, s * SPAN : (s + 1) * SPAN, :] = keys_of(index)
                zsend[k, d, 1, s * SPAN : (s + 1) * SPAN, :] = values_of(index)
            return 0

        lax.fori_loop(0, REQ, one, 0)

    def z_copy(k, i):
        d = lax.rem(z + i, REQ)
        return pltpu.make_async_remote_copy(
            src_ref=zsend.at[k, d],
            dst_ref=zrecv.at[k, z],
            send_sem=zs_sem.at[k, d],
            recv_sem=zr_sem.at[k, z],
            device_id=(d, c),
            device_id_type=MESH,
        )

    def z_arrival(k, i):
        s = lax.rem(z + i, REQ)
        return pltpu.make_async_remote_copy(
            src_ref=zsend.at[k, s],
            dst_ref=zrecv.at[k, s],
            send_sem=zs_sem.at[k, s],
            recv_sem=zr_sem.at[k, s],
            device_id=(s, c),
            device_id_type=MESH,
        )

    def q_send(source, to, sem):
        return pltpu.make_async_remote_copy(
            src_ref=query_all.at[source],
            dst_ref=query_all.at[source],
            send_sem=sem,
            recv_sem=qr_sem.at[source],
            device_id=(z, to),
            device_id_type=MESH,
        )

    def q_copy(to):
        return q_send(c, to, qs_sem.at[to])

    def q_forward(source):
        return q_send(source, sibling, qf_sem.at[source])

    def x_copy(k, half):
        return pltpu.make_async_remote_copy(
            src_ref=xsend.at[k, half],
            dst_ref=xrecv.at[k, half],
            send_sem=xs_sem.at[k, half],
            recv_sem=xr_sem.at[k, half],
            device_id=(z, sibling),
            device_id_type=MESH,
        )

    def r_copy(to_chip):
        spot = lax.rem(chip - to_chip // 2 * 2 + 2 * CHIPS - 2, CHIPS)
        return pltpu.make_async_remote_copy(
            src_ref=rsend.at[to_chip],
            dst_ref=rrecv.at[spot],
            send_sem=rs_sem.at[to_chip],
            recv_sem=rr_sem.at[spot],
            device_id=(z, to_chip * 2 + core),
            device_id_type=MESH,
        )

    def r_arrival(spot):
        from_chip = lax.rem(group * 2 + 2 + spot, CHIPS)
        return pltpu.make_async_remote_copy(
            src_ref=rsend.at[from_chip],
            dst_ref=rrecv.at[spot],
            send_sem=rs_sem.at[from_chip],
            recv_sem=rr_sem.at[spot],
            device_id=(z, from_chip * 2 + core),
            device_id_type=MESH,
        )

    def l_copy(to):
        return pltpu.make_async_remote_copy(
            src_ref=lsend.at[to],
            dst_ref=lrecv.at[place],
            send_sem=ls_sem.at[to],
            recv_sem=lr_sem.at[place],
            device_id=(z, group * OWNERS + to),
            device_id_type=MESH,
        )

    def l_arrival(source):
        return pltpu.make_async_remote_copy(
            src_ref=lsend.at[source],
            dst_ref=lrecv.at[source],
            send_sem=ls_sem.at[source],
            recv_sem=lr_sem.at[source],
            device_id=(z, group * OWNERS + source),
            device_id_type=MESH,
        )

    def send_stage(k):
        for i in (4, 3, 5, 2, 6, 1, 7):
            z_copy(k, i).start()

    load_keys.wait()
    load_values.wait()
    pack(0, lambda index: first_pieces[0, index], lambda index: first_pieces[1, index])
    pl.semaphore_wait(barrier, REQ - 1 + CHIPS + 1)
    send_stage(0)
    zrecv[0, z] = zsend[0, z]

    load_query.wait()
    query_all[c, 0:TOKENS, :] = query_in[:, 0:HEAD_SIZE]
    query_all[c, TOKENS:ROWS, :] = query_in[:, HEAD_SIZE : 2 * HEAD_SIZE]

    q_copy(sibling).start()

    def send_query(i, _):
        to = lax.rem(group + 2 * KEY_VALUE_HEADS - 1 - i // 2, KEY_VALUE_HEADS) * 2 + lax.rem(chip + i, 2)

        @pl.when(to != chip)
        def _():
            q_copy(to * 2 + core).start()

        return 0

    lax.fori_loop(0, CHIPS, send_query, 0)

    load_suffix.wait()

    def pack_and_send(k, _):
        key_at, value_at = columns(k)
        pack(k, lambda index: suffix[index, :, key_at], lambda index: suffix[index, :, value_at])
        send_stage(k)
        zrecv[k, z] = zsend[k, z]
        return 0

    lax.fori_loop(1, KEY_VALUE_HEADS, pack_and_send, 0)

    load_parents.wait()
    load_mask.wait()

    own = [roots[z * PER_REQ + j] >> 4 for j in range(PER_REQ)]
    for j in range(PER_REQ):
        rank = jnp.int32(0)
        for i in range(j):
            rank = rank + (own[i] == own[j]).astype(jnp.int32)
        slot[j] = own[j] * CAP + rank

    lane_slot = lax.broadcasted_iota(jnp.int32, (1, REQ * CAP * SPAN), 1) // SPAN
    lane_token = lax.rem(lax.broadcasted_iota(jnp.int32, (1, ROWS), 1), TOKENS)

    def trace(j, carry):
        lines = list(carry)
        for t in range(DRAFT_STEPS):
            at = j
            path = {t: at}
            for back in range(t - 1, -1, -1):
                at = parents[back, at]
                path[back] = at
            here = jnp.where(block_mask[group, at] > 0, slot[at], -1)
            mask[pl.ds(t * PER_REQ + j, 1), :] = jnp.where(lane_slot == here, 0.0, MASKED)
            for s in range(t + 1):
                lines[s] = jnp.where(lane_token == t * PER_REQ + j, path[s], lines[s])
        return tuple(lines)

    lines = lax.fori_loop(
        0, PER_REQ, trace, tuple(jnp.full((1, ROWS), -1, jnp.int32) for _ in range(DRAFT_STEPS))
    )

    load_prompt.wait()
    load_draft.wait()
    lane = lax.broadcasted_iota(jnp.int32, (ROWS, HEAD_SIZE), 1)

    def hand_on(k):
        for half in range(2):
            owner = head_of(k) * OWNERS + core + 2 * half

            @pl.when(owner != c)
            def _():
                q_send(owner, sibling, qf_sem.at[owner]).wait_recv()
                q_forward(owner).start()

    def weigh(scores, peak, values):
        weight = jnp.exp2((scores - peak) * EXP_SCALE)
        total = jnp.sum(weight, axis=1, keepdims=True)
        return total, jnp.dot(weight.astype(jnp.bfloat16), values, preferred_element_type=jnp.float32)

    def suffix_scores(k, rows):
        keys = zrecv[k, :, 0].reshape(REQ * CAP * SPAN, HEAD_SIZE)
        bias = mask[...]
        return nt_dot(rows, keys) + jnp.concatenate([bias, bias], axis=0)

    def suffix_values(k):
        return zrecv[k, :, 1].reshape(REQ * CAP * SPAN, HEAD_SIZE)

    def partial(k, owner):
        key_at, value_at = columns(k)
        rows = query_all[owner]
        score_prompt = nt_dot(rows, prompt[:, key_at])
        score_suffix = suffix_scores(k, rows)
        peak = jnp.maximum(
            jnp.max(score_prompt, axis=1, keepdims=True), jnp.max(score_suffix, axis=1, keepdims=True)
        )
        total_prompt, accum_prompt = weigh(score_prompt, peak, prompt[:, value_at])
        total_suffix, accum_suffix = weigh(score_suffix, peak, suffix_values(k))
        return accum_prompt + accum_suffix, jnp.where(lane == 0, peak, total_prompt + total_suffix)

    def wait_z(k):
        def one(i, _):
            z_arrival(k, i).wait_recv()
            return 0

        lax.fori_loop(1, REQ, one, 0)

    def combine(k):
        def one(half, _):
            to_chip = head_of(k) * 2 + half
            x_copy(k, half).wait_recv()
            peak_here, peak_there = keep[lax.rem(k, 2), half, ROWS : 2 * ROWS, 0:1], xrecv[k, half, ROWS : 2 * ROWS, 0:1]
            total_here, total_there = keep[lax.rem(k, 2), half, ROWS : 2 * ROWS, 1:2], xrecv[k, half, ROWS : 2 * ROWS, 1:2]
            peak = jnp.maximum(peak_here, peak_there)
            here = jnp.exp2((peak_here - peak) * EXP_SCALE)
            there = jnp.exp2((peak_there - peak) * EXP_SCALE)
            rsend[to_chip, 0:ROWS, :] = keep[lax.rem(k, 2), half, 0:ROWS, :] * here + xrecv[k, half, 0:ROWS, :] * there
            stats = jnp.transpose(jnp.where(lane == 0, peak, total_here * here + total_there * there))
            rsend[to_chip, ROWS : ROWS + STAT, :] = stats[0:STAT]

            r_copy(to_chip).start()
            return 0

        lax.fori_loop(0, 2, one, 0)

    def last_prompt(part):
        owner = group * OWNERS + part

        @pl.when(lax.rem(part, 2) != core)
        def _():
            q_send(owner, sibling, qf_sem.at[owner]).wait_recv()

        score_prompt = nt_dot(query_all[owner], prompt[:, columns(LAST)[0]])
        peak = jnp.max(score_prompt, axis=1, keepdims=True)
        total, accum = weigh(score_prompt, peak, prompt[:, columns(LAST)[1]])
        last_part[part, 0:ROWS, :] = accum
        last_part[part, ROWS : 2 * ROWS, :] = jnp.where(lane == 0, peak, total)

    def add_early():
        def wait_r(spot, _):
            r_arrival(spot).wait_recv()
            return 0

        lax.fori_loop(EARLY, CHIPS - 2, wait_r, 0)
        peaks = rrecv[EARLY : CHIPS - 2, ROWS, :]
        peak = jnp.max(peaks, axis=0, keepdims=True)
        factor = jnp.exp2((peaks - peak) * EXP_SCALE)
        total = jnp.sum(rrecv[EARLY : CHIPS - 2, ROWS + 1, :] * factor, axis=0, keepdims=True)
        turned = jnp.transpose(
            jnp.concatenate([factor, jnp.broadcast_to(total, (ROWS - CHIPS + 2 + EARLY, ROWS))], axis=0)
        )
        numerator = rrecv[EARLY, 0:ROWS, :] * turned[:, 0:1]
        for s in range(EARLY + 1, CHIPS - 2):
            numerator = numerator + rrecv[s, 0:ROWS, :] * turned[:, s - EARLY : s - EARLY + 1]
        base[0:ROWS, :] = numerator
        base[ROWS : ROWS + 1, :] = peak
        base[ROWS + 1 : ROWS + 2, :] = total

    def stage(k, _):
        @pl.when(k < LAST - 1)
        def _():
            hand_on(k + 1)

        @pl.when(k > 0)
        def _():
            combine(k - 1)

        @pl.when(k == 1)
        def _():
            hand_on(LAST)

        @pl.when((k > 1) & (k < 2 + OWNERS))
        def _():
            last_prompt(k - 2)

        @pl.when(k == LAST - 1)
        def _():
            add_early()

        wait_z(k)

        def give(half, _):
            owner = head_of(k) * OWNERS + 1 - core + 2 * half
            q_send(owner, sibling, qf_sem.at[owner]).wait_recv()
            accum, stats = partial(k, owner)
            xsend[k, half, 0:ROWS, :] = accum
            xsend[k, half, ROWS : 2 * ROWS, :] = stats
            x_copy(k, half).start()
            return 0

        lax.fori_loop(0, 2, give, 0)

        def hold(half, _):
            accum, stats = partial(k, head_of(k) * OWNERS + core + 2 * half)
            keep[lax.rem(k, 2), half, 0:ROWS, :] = accum
            keep[lax.rem(k, 2), half, ROWS : 2 * ROWS, :] = stats
            return 0

        lax.fori_loop(0, 2, hold, 0)

        return 0

    hand_on(0)
    lax.fori_loop(0, LAST, stage, 0)
    combine(LAST - 1)

    key_at, value_at = columns(LAST)

    score_draft = nt_dot(draft[:, key_at], query_all[c])
    particle = lax.broadcasted_iota(jnp.int32, (PER_REQ, ROWS), 0)
    allowed = jnp.concatenate([jnp.where(particle == line, 1, 0) for line in lines], axis=0)
    score_draft = jnp.where(allowed > 0, score_draft, MASKED)

    wait_z(LAST)

    def last_suffix(i, _):
        part = lax.rem(place + OWNERS - 1 - i, OWNERS)
        score_suffix = suffix_scores(LAST, query_all[group * OWNERS + part])
        peak_prompt, total_prompt = last_part[part, ROWS : 2 * ROWS, 0:1], last_part[part, ROWS : 2 * ROWS, 1:2]
        peak = jnp.maximum(peak_prompt, jnp.max(score_suffix, axis=1, keepdims=True))
        total, accum = weigh(score_suffix, peak, suffix_values(LAST))
        carried = jnp.exp2((peak_prompt - peak) * EXP_SCALE)
        lsend[part, 0:ROWS, :] = accum + last_part[part, 0:ROWS, :] * carried
        stats = jnp.transpose(jnp.where(lane == 0, peak, total + total_prompt * carried))
        lsend[part, ROWS : ROWS + STAT, :] = stats[0:STAT]

        @pl.when(part != place)
        def _():
            l_copy(part).start()

        return 0

    lax.fori_loop(0, OWNERS, last_suffix, 0)

    for spot in range(EARLY):
        r_arrival(spot).wait_recv()

    def drain_z(k):
        def one(i, _):
            z_copy(k, i).wait_send()
            return 0

        lax.fori_loop(1, REQ, one, 0)

    def drain_stage(k, _):
        drain_z(k)
        for half in range(2):
            x_copy(k, half).wait_send()
            r_copy(head_of(k) * 2 + half).wait_send()
        return 0

    lax.fori_loop(0, LAST, drain_stage, 0)

    def drain_chip(i, _):
        to = lax.rem(chip + i, CHIPS)
        q_copy(to * 2 + core).wait_send()
        q_forward(to * 2 + core).wait_send()
        return 0

    lax.fori_loop(1, CHIPS, drain_chip, 0)
    q_copy(sibling).wait_send()

    lrecv[place] = lsend[place]
    drain_z(LAST)
    for i in range(1, OWNERS):
        l_arrival(lax.rem(place + i, OWNERS)).wait_recv()

    base_peak, base_total = base[ROWS : ROWS + 1, :], base[ROWS + 1 : ROWS + 2, :]
    peaks = jnp.concatenate([lrecv[:, ROWS, :], rrecv[0:EARLY, ROWS, :], base_peak], axis=0)
    totals = jnp.concatenate([lrecv[:, ROWS + 1, :], rrecv[0:EARLY, ROWS + 1, :], base_total], axis=0)
    highest = jnp.maximum(jnp.max(peaks, axis=0, keepdims=True), jnp.max(score_draft, axis=0, keepdims=True))
    factor = jnp.exp2((peaks - highest) * EXP_SCALE)
    weight_draft = jnp.exp2((score_draft - highest) * EXP_SCALE)
    total = jnp.sum(totals * factor, axis=0, keepdims=True) + jnp.sum(weight_draft, axis=0, keepdims=True)
    count = OWNERS + EARLY + 1
    turned = jnp.transpose(
        jnp.concatenate([factor, jnp.broadcast_to(total, (TOKENS - count, ROWS)), weight_draft], axis=0)
    )
    numerator = jnp.dot(
        turned[:, TOKENS:].astype(jnp.bfloat16), draft[:, value_at], preferred_element_type=jnp.float32
    )
    for s in range(OWNERS):
        numerator = numerator + lrecv[s, 0:ROWS, :] * turned[:, s : s + 1]
    for s in range(EARLY):
        numerator = numerator + rrecv[s, 0:ROWS, :] * turned[:, OWNERS + s : OWNERS + s + 1]
    numerator = numerator + base[0:ROWS, :] * turned[:, count - 1 : count]
    result = (numerator / turned[:, count : count + 1]).astype(jnp.bfloat16)
    out_ref[:, 0:HEAD_SIZE] = result[0:TOKENS]
    out_ref[:, HEAD_SIZE : 2 * HEAD_SIZE] = result[TOKENS:ROWS]
    for i in range(1, OWNERS):
        l_copy(lax.rem(place + i, OWNERS)).wait_send()


def body(prompt_key_value, suffix_key_value, roots, parents, block_mask, queries, draft_kv):
    hbm = pl.BlockSpec(memory_space=pltpu.HBM)
    bf16, f32 = jnp.bfloat16, jnp.float32
    result = pl.pallas_call(
        kernel,
        out_shape=jax.ShapeDtypeStruct((TOKENS, 2 * HEAD_SIZE), bf16),
        in_specs=[hbm] * 7,
        out_specs=pl.BlockSpec(memory_space=pltpu.VMEM),
        scratch_shapes=[
            pltpu.VMEM((PROMPT, 2 * WIDTH), bf16),
            pltpu.VMEM((PER_REQ, SPAN, 2 * WIDTH), bf16),
            pltpu.VMEM((2, PER_REQ, SPAN, HEAD_SIZE), bf16),
            pltpu.VMEM((TOKENS, 2 * WIDTH), bf16),
            pltpu.VMEM((TOKENS, 2 * HEAD_SIZE), bf16),
            pltpu.VMEM((KEY_VALUE_HEADS, REQ, 2, CAP * SPAN, HEAD_SIZE), bf16),
            pltpu.VMEM((KEY_VALUE_HEADS, REQ, 2, CAP * SPAN, HEAD_SIZE), bf16),
            pltpu.VMEM((CTX, ROWS, HEAD_SIZE), bf16),
            pltpu.VMEM((LAST, 2, 2 * ROWS, HEAD_SIZE), f32),
            pltpu.VMEM((LAST, 2, 2 * ROWS, HEAD_SIZE), f32),
            pltpu.VMEM((2, 2, 2 * ROWS, HEAD_SIZE), f32),
            pltpu.VMEM((CHIPS, ROWS + STAT, HEAD_SIZE), f32),
            pltpu.VMEM((CHIPS - 2, ROWS + STAT, HEAD_SIZE), f32),
            pltpu.VMEM((OWNERS, 2 * ROWS, HEAD_SIZE), f32),
            pltpu.VMEM((OWNERS, ROWS + STAT, HEAD_SIZE), f32),
            pltpu.VMEM((OWNERS, ROWS + STAT, HEAD_SIZE), f32),
            pltpu.VMEM((ROWS + STAT, HEAD_SIZE), f32),
            pltpu.VMEM((TOKENS, REQ * CAP * SPAN), f32),
            pltpu.SMEM((REQ * PER_REQ,), jnp.int32),
            pltpu.SMEM((DRAFT_STEPS - 1, PER_REQ), jnp.int32),
            pltpu.SMEM((KEY_VALUE_HEADS, PER_REQ), jnp.int32),
            pltpu.SMEM((REQ * CAP,), jnp.int32),
            pltpu.SMEM((PER_REQ,), jnp.int32),
            pltpu.SemaphoreType.DMA((9,)),
            pltpu.SemaphoreType.DMA((KEY_VALUE_HEADS, REQ)),
            pltpu.SemaphoreType.DMA((KEY_VALUE_HEADS, REQ)),
            pltpu.SemaphoreType.DMA((CTX,)),
            pltpu.SemaphoreType.DMA((CTX,)),
            pltpu.SemaphoreType.DMA((CTX,)),
            pltpu.SemaphoreType.DMA((LAST, 2)),
            pltpu.SemaphoreType.DMA((LAST, 2)),
            pltpu.SemaphoreType.DMA((CHIPS,)),
            pltpu.SemaphoreType.DMA((CHIPS - 2,)),
            pltpu.SemaphoreType.DMA((OWNERS,)),
            pltpu.SemaphoreType.DMA((OWNERS,)),
        ],
        compiler_params=pltpu.CompilerParams(
            collective_id=0, has_side_effects=True, vmem_limit_bytes=48 * 1024 * 1024
        ),
        cost_estimate=pl.CostEstimate(flops=3_300_000_000, bytes_accessed=7_000_000, transcendentals=6_300_000),
    )(*(
        pltpu.with_memory_space_constraint(operand, pltpu.HBM)
        for operand in (
            roots,
            parents,
            block_mask.T,
            queries.reshape(TOKENS, 2 * HEAD_SIZE),
            draft_kv.reshape(TOKENS, 2 * WIDTH),
            prompt_key_value,
            suffix_key_value,
        )
    ))
    return result.reshape(DRAFT_STEPS, PER_REQ, 2 * HEAD_SIZE)


def solution(mesh):
    return jax.shard_map(
        body,
        mesh=mesh,
        in_specs=(
            P("ctx", None),
            P("req", "ctx", None),
            P(),
            P(None, "req"),
            P("req", None),
            P(None, "req", "ctx"),
            P(None, "req", None),
        ),
        out_specs=P(None, "req", "ctx"),
        check_vma=False,
    )
```

```python
import functools
import math

import jax
import jax.numpy as jnp
from jax import lax
from jax.experimental import pallas as pl
from jax.experimental.pallas import tpu as pltpu
from jax.sharding import PartitionSpec as P

MESH = pl.DeviceIdType.MESH

QUERY_HEAD_COUNT = 64
KEY_VALUE_HEADS = 8
HEAD_SIZE = 128
DRAFT_STEPS = 4
WIDTH = KEY_VALUE_HEADS * HEAD_SIZE
REQ = 8
CTX = 32
CHIPS = CTX // 2
LAST = KEY_VALUE_HEADS - 1
EARLY = 4
PER_REQ = 16
CAP = 2
SPAN = 32
PROMPT = 1024
TOKENS = DRAFT_STEPS * PER_REQ
ROWS = 2 * TOKENS
OWNERS = CTX // KEY_VALUE_HEADS
STAT = 8
MASKED = -1e30
EXP_SCALE = math.log2(math.e) / math.sqrt(HEAD_SIZE)


def nt_dot(a, b):
    return lax.dot_general(a, b, (((1,), (1,)), ((), ())), preferred_element_type=jnp.float32)


def kernel(
    roots_hbm, parents_hbm, mask_hbm, queries_hbm, draft_hbm, prompt_hbm, suffix_hbm, out_ref,
    prompt, suffix, first_pieces, draft, query_in, zsend, zrecv, query_all, xsend, xrecv, keep, rsend, rrecv,
    last_part, lsend, lrecv, base, mask,
    roots, parents, block_mask, pick, slot,
    load_sem, zs_sem, zr_sem, qs_sem, qf_sem, qr_sem, xs_sem, xr_sem, rs_sem, rr_sem, ls_sem, lr_sem,
):
    z = lax.axis_index("req")
    c = lax.axis_index("ctx")
    group = c // OWNERS
    chip = c // 2
    core = lax.rem(c, 2)
    sibling = chip * 2 + 1 - core
    place = lax.rem(c, OWNERS)
    across = group * OWNERS + OWNERS - 1 - place

    def head_of(k):
        return lax.rem(group + 1 + k, KEY_VALUE_HEADS)

    def columns(k):
        key_at = pl.ds(pl.multiple_of(head_of(k) * HEAD_SIZE, HEAD_SIZE), HEAD_SIZE)
        value_at = pl.ds(pl.multiple_of(WIDTH + head_of(k) * HEAD_SIZE, HEAD_SIZE), HEAD_SIZE)
        return key_at, value_at

    load_roots = pltpu.make_async_copy(roots_hbm, roots, load_sem.at[0])
    load_roots.start()
    key_at, value_at = columns(0)
    load_keys = pltpu.make_async_copy(suffix_hbm.at[:, :, key_at], first_pieces.at[0], load_sem.at[1])
    load_values = pltpu.make_async_copy(suffix_hbm.at[:, :, value_at], first_pieces.at[1], load_sem.at[2])
    load_keys.start()
    load_values.start()

    barrier = pltpu.get_barrier_semaphore()

    def greet_z(i, _):
        pl.semaphore_signal(barrier, inc=1, device_id=(lax.rem(z + i, REQ), c), device_id_type=MESH)
        return 0

    def greet_chip(i, _):
        to = lax.rem(chip + i, CHIPS) * 2 + core
        pl.semaphore_signal(barrier, inc=1, device_id=(z, to), device_id_type=MESH)
        return 0

    lax.fori_loop(1, REQ, greet_z, 0)
    lax.fori_loop(1, CHIPS, greet_chip, 0)
    pl.semaphore_signal(barrier, inc=1, device_id=(z, sibling), device_id_type=MESH)
    pl.semaphore_signal(barrier, inc=1, device_id=(z, across), device_id_type=MESH)

    load_query = pltpu.make_async_copy(queries_hbm, query_in, load_sem.at[3])
    load_suffix = pltpu.make_async_copy(suffix_hbm, suffix, load_sem.at[4])
    load_parents = pltpu.make_async_copy(parents_hbm, parents, load_sem.at[5])
    load_mask = pltpu.make_async_copy(mask_hbm, block_mask, load_sem.at[6])
    load_prompt = pltpu.make_async_copy(prompt_hbm, prompt, load_sem.at[7])
    load_draft = pltpu.make_async_copy(draft_hbm, draft, load_sem.at[8])
    load_query.start()
    load_parents.start()
    load_mask.start()

    def choose(d, _):
        count, first, second = jnp.int32(0), jnp.int32(0), jnp.int32(0)
        for j in range(PER_REQ):
            root = roots[d * PER_REQ + j]
            mine = (root >> 4) == z
            local = root & 15
            first = jnp.where(mine & (count == 0), local, first)
            second = jnp.where(mine & (count == 1), local, second)
            count = count + mine.astype(jnp.int32)
        pick[2 * d] = first
        pick[2 * d + 1] = second
        return 0

    load_roots.wait()
    lax.fori_loop(0, REQ, choose, 0)

    def pack(k, keys_of, values_of):
        def one(d, _):
            for s in range(CAP):
                index = pick[2 * d + s]
                zsend[k, d, 0, s * SPAN : (s + 1) * SPAN, :] = keys_of(index)
                zsend[k, d, 1, s * SPAN : (s + 1) * SPAN, :] = values_of(index)
            return 0

        lax.fori_loop(0, REQ, one, 0)

    def z_copy(k, i):
        d = lax.rem(z + i, REQ)
        return pltpu.make_async_remote_copy(
            src_ref=zsend.at[k, d],
            dst_ref=zrecv.at[k, z],
            send_sem=zs_sem.at[k, d],
            recv_sem=zr_sem.at[k, z],
            device_id=(d, c),
            device_id_type=MESH,
        )

    def z_arrival(k, i):
        s = lax.rem(z + i, REQ)
        return pltpu.make_async_remote_copy(
            src_ref=zsend.at[k, s],
            dst_ref=zrecv.at[k, s],
            send_sem=zs_sem.at[k, s],
            recv_sem=zr_sem.at[k, s],
            device_id=(s, c),
            device_id_type=MESH,
        )

    def q_send(source, to, sem):
        return pltpu.make_async_remote_copy(
            src_ref=query_all.at[source],
            dst_ref=query_all.at[source],
            send_sem=sem,
            recv_sem=qr_sem.at[source],
            device_id=(z, to),
            device_id_type=MESH,
        )

    def q_copy(to):
        return q_send(c, to, qs_sem.at[to])

    def q_forward(source):
        return q_send(source, sibling, qf_sem.at[source])

    def x_copy(k, half):
        return pltpu.make_async_remote_copy(
            src_ref=xsend.at[k, half],
            dst_ref=xrecv.at[k, half],
            send_sem=xs_sem.at[k, half],
            recv_sem=xr_sem.at[k, half],
            device_id=(z, sibling),
            device_id_type=MESH,
        )

    def r_copy(to_chip):
        spot = lax.rem(chip - to_chip // 2 * 2 + 2 * CHIPS - 2, CHIPS)
        return pltpu.make_async_remote_copy(
            src_ref=rsend.at[to_chip],
            dst_ref=rrecv.at[spot],
            send_sem=rs_sem.at[to_chip],
            recv_sem=rr_sem.at[spot],
            device_id=(z, to_chip * 2 + core),
            device_id_type=MESH,
        )

    def r_arrival(spot):
        from_chip = lax.rem(group * 2 + 2 + spot, CHIPS)
        return pltpu.make_async_remote_copy(
            src_ref=rsend.at[from_chip],
            dst_ref=rrecv.at[spot],
            send_sem=rs_sem.at[from_chip],
            recv_sem=rr_sem.at[spot],
            device_id=(z, from_chip * 2 + core),
            device_id_type=MESH,
        )

    def l_copy(to):
        return pltpu.make_async_remote_copy(
            src_ref=lsend.at[to],
            dst_ref=lrecv.at[place],
            send_sem=ls_sem.at[to],
            recv_sem=lr_sem.at[place],
            device_id=(z, group * OWNERS + to),
            device_id_type=MESH,
        )

    def l_arrival(source):
        return pltpu.make_async_remote_copy(
            src_ref=lsend.at[source],
            dst_ref=lrecv.at[source],
            send_sem=ls_sem.at[source],
            recv_sem=lr_sem.at[source],
            device_id=(z, group * OWNERS + source),
            device_id_type=MESH,
        )

    def send_stage(k):
        for i in (4, 3, 5, 2, 6, 1, 7):
            z_copy(k, i).start()

    load_keys.wait()
    load_values.wait()
    pack(0, lambda index: first_pieces[0, index], lambda index: first_pieces[1, index])
    pl.semaphore_wait(barrier, REQ - 1 + CHIPS + 1)
    send_stage(0)
    load_suffix.start()
    load_prompt.start()
    load_draft.start()
    zrecv[0, z] = zsend[0, z]

    load_query.wait()
    query_all[c, 0:TOKENS, :] = query_in[:, 0:HEAD_SIZE]
    query_all[c, TOKENS:ROWS, :] = query_in[:, HEAD_SIZE : 2 * HEAD_SIZE]

    q_copy(sibling).start()

    def send_query(i, _):
        to = lax.rem(group + 2 * KEY_VALUE_HEADS - 1 - i // 2, KEY_VALUE_HEADS) * 2 + lax.rem(chip + i, 2)

        @pl.when(to != chip)
        def _():
            q_copy(to * 2 + core).start()

        return 0

    lax.fori_loop(0, CHIPS, send_query, 0)

    load_suffix.wait()

    def pack_and_send(k, _):
        key_at, value_at = columns(k)
        pack(k, lambda index: suffix[index, :, key_at], lambda index: suffix[index, :, value_at])
        send_stage(k)
        zrecv[k, z] = zsend[k, z]
        return 0

    lax.fori_loop(1, KEY_VALUE_HEADS, pack_and_send, 0)

    load_parents.wait()
    load_mask.wait()

    own = [roots[z * PER_REQ + j] >> 4 for j in range(PER_REQ)]
    for j in range(PER_REQ):
        rank = jnp.int32(0)
        for i in range(j):
            rank = rank + (own[i] == own[j]).astype(jnp.int32)
        slot[j] = own[j] * CAP + rank

    lane_slot = lax.broadcasted_iota(jnp.int32, (1, REQ * CAP * SPAN), 1) // SPAN
    lane_token = lax.rem(lax.broadcasted_iota(jnp.int32, (1, ROWS), 1), TOKENS)

    def trace(j, carry):
        lines = list(carry)
        for t in range(DRAFT_STEPS):
            at = j
            path = {t: at}
            for back in range(t - 1, -1, -1):
                at = parents[back, at]
                path[back] = at
            here = jnp.where(block_mask[group, at] > 0, slot[at], -1)
            mask[pl.ds(t * PER_REQ + j, 1), :] = jnp.where(lane_slot == here, 0.0, MASKED)
            for s in range(t + 1):
                lines[s] = jnp.where(lane_token == t * PER_REQ + j, path[s], lines[s])
        return tuple(lines)

    lines = lax.fori_loop(
        0, PER_REQ, trace, tuple(jnp.full((1, ROWS), -1, jnp.int32) for _ in range(DRAFT_STEPS))
    )

    load_prompt.wait()
    load_draft.wait()
    lane = lax.broadcasted_iota(jnp.int32, (ROWS, HEAD_SIZE), 1)

    def hand_on(k):
        for half in range(2):
            owner = head_of(k) * OWNERS + core + 2 * half

            @pl.when(owner != c)
            def _():
                q_send(owner, sibling, qf_sem.at[owner]).wait_recv()
                q_forward(owner).start()

    def weigh(scores, peak, values):
        weight = jnp.exp2((scores - peak) * EXP_SCALE)
        total = jnp.sum(weight, axis=1, keepdims=True)
        return total, jnp.dot(weight.astype(jnp.bfloat16), values, preferred_element_type=jnp.float32)

    def suffix_scores(k, rows):
        keys = zrecv[k, :, 0].reshape(REQ * CAP * SPAN, HEAD_SIZE)
        bias = mask[...]
        return nt_dot(rows, keys) + jnp.concatenate([bias, bias], axis=0)

    def suffix_values(k):
        return zrecv[k, :, 1].reshape(REQ * CAP * SPAN, HEAD_SIZE)

    def partial(k, owner):
        key_at, value_at = columns(k)
        rows = query_all[owner]
        score_prompt = nt_dot(rows, prompt[:, key_at])
        score_suffix = suffix_scores(k, rows)
        peak = jnp.maximum(
            jnp.max(score_prompt, axis=1, keepdims=True), jnp.max(score_suffix, axis=1, keepdims=True)
        )
        total_prompt, accum_prompt = weigh(score_prompt, peak, prompt[:, value_at])
        total_suffix, accum_suffix = weigh(score_suffix, peak, suffix_values(k))
        return accum_prompt + accum_suffix, jnp.where(lane == 0, peak, total_prompt + total_suffix)

    def wait_z(k):
        def one(i, _):
            z_arrival(k, i).wait_recv()
            return 0

        lax.fori_loop(1, REQ, one, 0)

    def combine(k):
        def one(half, _):
            to_chip = head_of(k) * 2 + half
            x_copy(k, half).wait_recv()
            peak_here, peak_there = keep[lax.rem(k, 2), half, ROWS : 2 * ROWS, 0:1], xrecv[k, half, ROWS : 2 * ROWS, 0:1]
            total_here, total_there = keep[lax.rem(k, 2), half, ROWS : 2 * ROWS, 1:2], xrecv[k, half, ROWS : 2 * ROWS, 1:2]
            peak = jnp.maximum(peak_here, peak_there)
            here = jnp.exp2((peak_here - peak) * EXP_SCALE)
            there = jnp.exp2((peak_there - peak) * EXP_SCALE)
            rsend[to_chip, 0:ROWS, :] = keep[lax.rem(k, 2), half, 0:ROWS, :] * here + xrecv[k, half, 0:ROWS, :] * there
            stats = jnp.transpose(jnp.where(lane == 0, peak, total_here * here + total_there * there))
            rsend[to_chip, ROWS : ROWS + STAT, :] = stats[0:STAT]

            r_copy(to_chip).start()
            return 0

        lax.fori_loop(0, 2, one, 0)

    def last_prompt(part):
        owner = group * OWNERS + part

        @pl.when(lax.rem(part, 2) != core)
        def _():
            q_send(owner, sibling, qf_sem.at[owner]).wait_recv()

        score_prompt = nt_dot(query_all[owner], prompt[:, columns(LAST)[0]])
        peak = jnp.max(score_prompt, axis=1, keepdims=True)
        total, accum = weigh(score_prompt, peak, prompt[:, columns(LAST)[1]])
        last_part[part, 0:ROWS, :] = accum
        last_part[part, ROWS : 2 * ROWS, :] = jnp.where(lane == 0, peak, total)

    def add_early():
        def wait_r(spot, _):
            r_arrival(spot).wait_recv()
            return 0

        lax.fori_loop(EARLY, CHIPS - 2, wait_r, 0)
        peaks = rrecv[EARLY : CHIPS - 2, ROWS, :]
        peak = jnp.max(peaks, axis=0, keepdims=True)
        factor = jnp.exp2((peaks - peak) * EXP_SCALE)
        total = jnp.sum(rrecv[EARLY : CHIPS - 2, ROWS + 1, :] * factor, axis=0, keepdims=True)
        turned = jnp.transpose(
            jnp.concatenate([factor, jnp.broadcast_to(total, (ROWS - CHIPS + 2 + EARLY, ROWS))], axis=0)
        )
        numerator = rrecv[EARLY, 0:ROWS, :] * turned[:, 0:1]
        for s in range(EARLY + 1, CHIPS - 2):
            numerator = numerator + rrecv[s, 0:ROWS, :] * turned[:, s - EARLY : s - EARLY + 1]
        base[0:ROWS, :] = numerator
        base[ROWS : ROWS + 1, :] = peak
        base[ROWS + 1 : ROWS + 2, :] = total

    def stage(k, _):
        @pl.when(k < LAST - 1)
        def _():
            hand_on(k + 1)

        @pl.when(k > 0)
        def _():
            combine(k - 1)

        @pl.when(k == 1)
        def _():
            hand_on(LAST)

        @pl.when((k > 1) & (k < 2 + OWNERS))
        def _():
            last_prompt(k - 2)

        @pl.when(k == LAST - 1)
        def _():
            add_early()

        wait_z(k)

        def give(half, _):
            owner = head_of(k) * OWNERS + 1 - core + 2 * half
            q_send(owner, sibling, qf_sem.at[owner]).wait_recv()
            accum, stats = partial(k, owner)
            xsend[k, half, 0:ROWS, :] = accum
            xsend[k, half, ROWS : 2 * ROWS, :] = stats
            x_copy(k, half).start()
            return 0

        lax.fori_loop(0, 2, give, 0)

        def hold(half, _):
            accum, stats = partial(k, head_of(k) * OWNERS + core + 2 * half)
            keep[lax.rem(k, 2), half, 0:ROWS, :] = accum
            keep[lax.rem(k, 2), half, ROWS : 2 * ROWS, :] = stats
            return 0

        lax.fori_loop(0, 2, hold, 0)

        return 0

    hand_on(0)
    lax.fori_loop(0, LAST, stage, 0)
    combine(LAST - 1)

    key_at, value_at = columns(LAST)

    score_draft = nt_dot(draft[:, key_at], query_all[c])
    particle = lax.broadcasted_iota(jnp.int32, (PER_REQ, ROWS), 0)
    allowed = jnp.concatenate([jnp.where(particle == line, 1, 0) for line in lines], axis=0)
    score_draft = jnp.where(allowed > 0, score_draft, MASKED)

    wait_z(LAST)

    def last_suffix(i, _):
        part = lax.rem(place + OWNERS - 1 - i, OWNERS)
        score_suffix = suffix_scores(LAST, query_all[group * OWNERS + part])
        peak_prompt, total_prompt = last_part[part, ROWS : 2 * ROWS, 0:1], last_part[part, ROWS : 2 * ROWS, 1:2]
        peak = jnp.maximum(peak_prompt, jnp.max(score_suffix, axis=1, keepdims=True))
        total, accum = weigh(score_suffix, peak, suffix_values(LAST))
        carried = jnp.exp2((peak_prompt - peak) * EXP_SCALE)
        lsend[part, 0:ROWS, :] = accum + last_part[part, 0:ROWS, :] * carried
        stats = jnp.transpose(jnp.where(lane == 0, peak, total + total_prompt * carried))
        lsend[part, ROWS : ROWS + STAT, :] = stats[0:STAT]

        @pl.when(part != place)
        def _():
            l_copy(part).start()

        return 0

    lax.fori_loop(0, OWNERS, last_suffix, 0)

    for spot in range(EARLY):
        r_arrival(spot).wait_recv()

    def drain_z(k):
        def one(i, _):
            z_copy(k, i).wait_send()
            return 0

        lax.fori_loop(1, REQ, one, 0)

    def drain_stage(k, _):
        drain_z(k)
        for half in range(2):
            x_copy(k, half).wait_send()
            r_copy(head_of(k) * 2 + half).wait_send()
        return 0

    lax.fori_loop(0, LAST, drain_stage, 0)

    def drain_chip(i, _):
        to = lax.rem(chip + i, CHIPS)
        q_copy(to * 2 + core).wait_send()
        q_forward(to * 2 + core).wait_send()
        return 0

    lax.fori_loop(1, CHIPS, drain_chip, 0)
    q_copy(sibling).wait_send()

    lrecv[place] = lsend[place]
    drain_z(LAST)
    for i in range(1, OWNERS):
        l_arrival(lax.rem(place + i, OWNERS)).wait_recv()

    base_peak, base_total = base[ROWS : ROWS + 1, :], base[ROWS + 1 : ROWS + 2, :]
    peaks = jnp.concatenate([lrecv[:, ROWS, :], rrecv[0:EARLY, ROWS, :], base_peak], axis=0)
    totals = jnp.concatenate([lrecv[:, ROWS + 1, :], rrecv[0:EARLY, ROWS + 1, :], base_total], axis=0)
    highest = jnp.maximum(jnp.max(peaks, axis=0, keepdims=True), jnp.max(score_draft, axis=0, keepdims=True))
    factor = jnp.exp2((peaks - highest) * EXP_SCALE)
    weight_draft = jnp.exp2((score_draft - highest) * EXP_SCALE)
    total = jnp.sum(totals * factor, axis=0, keepdims=True) + jnp.sum(weight_draft, axis=0, keepdims=True)
    count = OWNERS + EARLY + 1
    turned = jnp.transpose(
        jnp.concatenate([factor, jnp.broadcast_to(total, (TOKENS - count, ROWS)), weight_draft], axis=0)
    )
    numerator = jnp.dot(
        turned[:, TOKENS:].astype(jnp.bfloat16), draft[:, value_at], preferred_element_type=jnp.float32
    )
    for s in range(OWNERS):
        numerator = numerator + lrecv[s, 0:ROWS, :] * turned[:, s : s + 1]
    for s in range(EARLY):
        numerator = numerator + rrecv[s, 0:ROWS, :] * turned[:, OWNERS + s : OWNERS + s + 1]
    numerator = numerator + base[0:ROWS, :] * turned[:, count - 1 : count]
    result = (numerator / turned[:, count : count + 1]).astype(jnp.bfloat16)
    out_ref[:, 0:HEAD_SIZE] = result[0:TOKENS]
    out_ref[:, HEAD_SIZE : 2 * HEAD_SIZE] = result[TOKENS:ROWS]
    for i in range(1, OWNERS):
        l_copy(lax.rem(place + i, OWNERS)).wait_send()


def body(prompt_key_value, suffix_key_value, roots, parents, block_mask, queries, draft_kv):
    hbm = pl.BlockSpec(memory_space=pltpu.HBM)
    bf16, f32 = jnp.bfloat16, jnp.float32
    result = pl.pallas_call(
        kernel,
        out_shape=jax.ShapeDtypeStruct((TOKENS, 2 * HEAD_SIZE), bf16),
        in_specs=[hbm] * 7,
        out_specs=pl.BlockSpec(memory_space=pltpu.VMEM),
        scratch_shapes=[
            pltpu.VMEM((PROMPT, 2 * WIDTH), bf16),
            pltpu.VMEM((PER_REQ, SPAN, 2 * WIDTH), bf16),
            pltpu.VMEM((2, PER_REQ, SPAN, HEAD_SIZE), bf16),
            pltpu.VMEM((TOKENS, 2 * WIDTH), bf16),
            pltpu.VMEM((TOKENS, 2 * HEAD_SIZE), bf16),
            pltpu.VMEM((KEY_VALUE_HEADS, REQ, 2, CAP * SPAN, HEAD_SIZE), bf16),
            pltpu.VMEM((KEY_VALUE_HEADS, REQ, 2, CAP * SPAN, HEAD_SIZE), bf16),
            pltpu.VMEM((CTX, ROWS, HEAD_SIZE), bf16),
            pltpu.VMEM((LAST, 2, 2 * ROWS, HEAD_SIZE), f32),
            pltpu.VMEM((LAST, 2, 2 * ROWS, HEAD_SIZE), f32),
            pltpu.VMEM((2, 2, 2 * ROWS, HEAD_SIZE), f32),
            pltpu.VMEM((CHIPS, ROWS + STAT, HEAD_SIZE), f32),
            pltpu.VMEM((CHIPS - 2, ROWS + STAT, HEAD_SIZE), f32),
            pltpu.VMEM((OWNERS, 2 * ROWS, HEAD_SIZE), f32),
            pltpu.VMEM((OWNERS, ROWS + STAT, HEAD_SIZE), f32),
            pltpu.VMEM((OWNERS, ROWS + STAT, HEAD_SIZE), f32),
            pltpu.VMEM((ROWS + STAT, HEAD_SIZE), f32),
            pltpu.VMEM((TOKENS, REQ * CAP * SPAN), f32),
            pltpu.SMEM((REQ * PER_REQ,), jnp.int32),
            pltpu.SMEM((DRAFT_STEPS - 1, PER_REQ), jnp.int32),
            pltpu.SMEM((KEY_VALUE_HEADS, PER_REQ), jnp.int32),
            pltpu.SMEM((REQ * CAP,), jnp.int32),
            pltpu.SMEM((PER_REQ,), jnp.int32),
            pltpu.SemaphoreType.DMA((9,)),
            pltpu.SemaphoreType.DMA((KEY_VALUE_HEADS, REQ)),
            pltpu.SemaphoreType.DMA((KEY_VALUE_HEADS, REQ)),
            pltpu.SemaphoreType.DMA((CTX,)),
            pltpu.SemaphoreType.DMA((CTX,)),
            pltpu.SemaphoreType.DMA((CTX,)),
            pltpu.SemaphoreType.DMA((LAST, 2)),
            pltpu.SemaphoreType.DMA((LAST, 2)),
            pltpu.SemaphoreType.DMA((CHIPS,)),
            pltpu.SemaphoreType.DMA((CHIPS - 2,)),
            pltpu.SemaphoreType.DMA((OWNERS,)),
            pltpu.SemaphoreType.DMA((OWNERS,)),
        ],
        compiler_params=pltpu.CompilerParams(
            collective_id=0, has_side_effects=True, vmem_limit_bytes=48 * 1024 * 1024
        ),
        cost_estimate=pl.CostEstimate(flops=3_300_000_000, bytes_accessed=7_000_000, transcendentals=6_300_000),
    )(*(
        pltpu.with_memory_space_constraint(operand, pltpu.HBM)
        for operand in (
            roots,
            parents,
            block_mask.T,
            queries.reshape(TOKENS, 2 * HEAD_SIZE),
            draft_kv.reshape(TOKENS, 2 * WIDTH),
            prompt_key_value,
            suffix_key_value,
        )
    ))
    return result.reshape(DRAFT_STEPS, PER_REQ, 2 * HEAD_SIZE)


def solution(mesh):
    return jax.shard_map(
        body,
        mesh=mesh,
        in_specs=(
            P("ctx", None),
            P("req", "ctx", None),
            P(),
            P(None, "req"),
            P("req", None),
            P(None, "req", "ctx"),
            P(None, "req", None),
        ),
        out_specs=P(None, "req", "ctx"),
        check_vma=False,
    )
```
